32 devices in a mesh: lat: 8 (over z, y), lon: 4 (over x, core).
Axes of the slice: x: 2, y: 2, z: 4, core: 2. Of those that a mesh axis runs over, the one named last changes fastest.
Arguments:
- adj_in: float32 [16, 32, 128, 512], P(None, 'lon', 'lat'), may hold values from -6 to 6
- courant_lon: float32 [32, 128, 512], P(None, 'lat', 'lon'), may hold values from 0.2 to 0.95
- courant_lat: float32 [32, 128, 512], P(None, 'lat', 'lon'), may hold values from 0.1 to 0.9
- mass: float32 [32, 128, 512], P(None, 'lat', 'lon'), may hold values from 0.3 to 3
- entrain: float32 [128, 512], P('lat', 'lon'), may hold values from 0.2 to 0.9
- cloud: int32 [2, 128, 512], P(None, 'lat', 'lon'), may hold values from 0 to 31, as said below
- substeps: int32 [128], P('lat'), may hold values from 1 to 8
Outputs:
- adj_out: float32 [16, 32, 128, 512], P(None, None, 'lat', 'lon')
The draws below stay inside these ranges and needn't reach their ends.
Inputs may be any that keep to these rules, and one draw needn't show every extreme that they name: cloud[0] <= cloud[1] in every column.
All inputs are finite; a program needn't handle non-finite values.
Results may differ from the reference program's by a relative error of at most 0.0001.
Values sent between devices are 32-bit elements; how exact they have to be, the bound alone decides.
No kernel may reach another device: no remote copies, remote signals or barrier semaphores. Data moves between devices by JAX's collectives and lax.ppermute only.
A program may use at most 128 MiB of HBM per device.

```python
import math
import jax
import jax.numpy as jnp
from jax import lax

K = 16
L = 32
MAXSUB = 8
NLAT = 128
NLON = 512


def draw_cloud(key, part):
    key_base = jax.random.fold_in(key, 11)
    key_depth = jax.random.fold_in(key, 12)
    base_level = jax.random.randint(key_base, (NLAT, NLON), 0, L // 2)
    depth_level = jax.random.randint(key_depth, (NLAT, NLON), 0, L // 2 + 1)
    base_level = base_level.at[0, 0].set(L // 2 - 1).at[0, 1].set(0)
    depth_level = depth_level.at[0, 0].set(L // 2)
    return jnp.stack([base_level, base_level + depth_level]).astype(jnp.int32)


def draw_substeps(key, part):
    latitude = jnp.arange(NLAT, dtype=jnp.int32)
    distance = jnp.abs(2 * latitude - (NLAT - 1))
    upper_count = 1 + (MAXSUB - 1) * distance // max(NLAT - 1, 1)
    counts = jax.random.randint(jax.random.fold_in(key, 21), (NLAT,), 1, upper_count + 1)
    counts = counts.at[0].set(MAXSUB).at[NLAT - 1].set(MAXSUB)
    return counts.astype(jnp.int32)


def shard_levels(stream_key, extent, cuts, low, largest):
    def one(dim, blocks):
        steps = jax.random.uniform(jax.random.fold_in(jax.random.fold_in(stream_key, 6), dim), (blocks,), jnp.float32, low / len(cuts), largest / len(cuts))
        return jnp.repeat(jnp.exp(steps), extent[dim] // blocks).reshape((-1,) + (1,) * (len(extent) - dim - 1))

    level = one(*cuts[0])
    for cut in cuts[1:]:
        level = level * one(*cut)
    return level


def centred(key, extent, spread, bound, cuts=(), kind=jnp.bfloat16):
    loudness = shard_levels(key, extent, cuts, -0.22, 0.18) if cuts else 1.0
    drawn = jax.random.normal(key, extent, jnp.float32) * spread * loudness
    return jnp.minimum(jnp.maximum(drawn, -bound), bound).astype(kind)


def setup_inputs(seed: int = 0) -> dict:
    arg_keys = jax.random.split(jax.random.key(seed), 8)
    adj_in = centred(arg_keys[0], (K, L, NLAT, NLON), 1.0, 6.0, ((1, 4), (2, 8)), jnp.float32)
    courant_lon = jnp.clip(0.2 + 0.75 * jax.random.uniform(arg_keys[1], (L, NLAT, NLON), jnp.float32) ** shard_levels(arg_keys[1], (L, NLAT, NLON), ((1, 8), (2, 4)), -0.2, 0.2), 0.2, 0.95)
    courant_lat = jnp.clip(0.1 + 0.79999997 * jax.random.uniform(arg_keys[2], (L, NLAT, NLON), jnp.float32) ** shard_levels(arg_keys[2], (L, NLAT, NLON), ((1, 8), (2, 4)), -0.2, 0.2), 0.1, 0.9)
    mass = jnp.clip(jnp.exp(math.log(3.0) - 2.3025851 * jax.random.uniform(arg_keys[3], (L, NLAT, NLON), jnp.float32) ** shard_levels(arg_keys[3], (L, NLAT, NLON), ((1, 8), (2, 4)), -0.2, 0.2)), 0.3, 3.0)
    entrain = jnp.clip(0.2 + 0.7 * jax.random.uniform(arg_keys[4], (NLAT, NLON), jnp.float32) ** shard_levels(arg_keys[4], (NLAT, NLON), ((0, 8), (1, 4)), -0.2, 0.2), 0.2, 0.9)
    cloud = draw_cloud(jax.random.fold_in(arg_keys[7], 71), 0)
    substeps = draw_substeps(jax.random.fold_in(arg_keys[7], 71), 0)
    return dict(adj_in=adj_in, courant_lon=courant_lon, courant_lat=courant_lat, mass=mass, entrain=entrain, cloud=cloud, substeps=substeps)


def advect_component(field, courant_lon, north_rate, substeps):
    def sweep_once(index, state):
        active = (index < substeps).astype(jnp.float32)[None, :, None]
        following = jnp.roll(state, -1, axis=2)
        return state + active * courant_lon * (following - state)

    field = lax.fori_loop(0, MAXSUB, sweep_once, field)
    following = jnp.concatenate([field[:, 1:, :], jnp.zeros_like(field[:, :1, :])], axis=1)
    return field + north_rate * (following - field)


def reference(adj_in, courant_lon, courant_lat, mass, entrain, cloud, substeps):
    latitude = jnp.arange(NLAT)
    north_rate = courant_lat * (latitude < NLAT - 1).astype(jnp.float32)[None, :, None]
    levels = jnp.arange(L)[:, None, None]
    inside = ((levels >= cloud[0]) & (levels <= cloud[1])).astype(jnp.float32)
    column_mass = jnp.sum(inside * mass, axis=0)
    detrain = entrain * inside * mass / column_mass
    keep_share = 1.0 - entrain * inside

    def one_component(field):
        moved = advect_component(field, courant_lon, north_rate, substeps)
        column_sum = jnp.sum(inside * moved, axis=0)
        return keep_share * moved + detrain * column_sum

    return lax.map(one_component, adj_in)
```

```python
import jax
import jax.numpy as jnp
from jax import lax
from jax.experimental import pallas as pl
from jax.experimental.pallas import tpu as pltpu
from jax.sharding import PartitionSpec as P

MAXSUB = 8
HALF = 8
VMEM_LIMIT = 48 * 1024 * 1024


def sent_east(block, distance):
    n = lax.axis_size("lon")
    return lax.ppermute(block, "lon", [(i, (i + distance) % n) for i in range(n)])


def sent_south(block):
    n = lax.axis_size("lat")
    return lax.ppermute(block, "lat", [(i + 1, i) for i in range(n - 1)])


def call(kernel, grid, in_specs, out_specs, out_shape, operands, scalars, elements, aliases=None, scratch=()):
    return pl.pallas_call(
        kernel,
        grid_spec=pltpu.PrefetchScalarGridSpec(
            num_scalar_prefetch=1, grid=grid, in_specs=in_specs, out_specs=out_specs, scratch_shapes=scratch
        ),
        out_shape=out_shape,
        input_output_aliases=aliases or {},
        compiler_params=pltpu.CompilerParams(vmem_limit_bytes=VMEM_LIMIT),
        cost_estimate=pl.CostEstimate(flops=elements * 20, bytes_accessed=elements * 8, transcendentals=0),
    )(scalars, *operands)


def sweep(me, adj, rates, active, moments, step, level_block, skip, row_block):
    n = len(rates)
    width = rates[0].shape[2]
    first, count = moments
    levels = rates[0].shape[0]
    rows = row_block[1]

    def kernel(me_ref, *refs):
        fields, cs, act, outs = refs[:n], refs[n : 2 * n], refs[2 * n], refs[2 * n + 1 :]
        last = lax.broadcasted_iota(jnp.int32, (levels, HALF, width), 2) == width - 1

        def one(m, carry):
            for g in range(rows // HALF):
                part = slice(g * HALF, (g + 1) * HALF)
                steps = jnp.broadcast_to(act[part, :][None], (levels, HALF, width))
                state = [f[m, skip : skip + levels, part, :] for f in fields]
                for s in range(MAXSUB):
                    rolled = [pltpu.roll(a, width - 1, 2) for a in state]
                    state = [
                        a
                        + jnp.where(steps > s, c[:, part, :], 0.0)
                        * (jnp.where(last, rolled[(r + 1) % n], rolled[r]) - a)
                        for r, (a, c) in enumerate(zip(state, cs))
                    ]
                for a, o in zip(state, outs):
                    o[m, :, part, :] = a
            return carry

        lax.fori_loop(0, step, one, 0)

    def tile(r):
        return pl.BlockSpec(
            (step, level_block, rows, width),
            lambda i, me, r=r: (i + first // step, 0, row_block[0], lax.rem(me[0] + r, n)),
        )

    in_specs = [tile(r) for r in range(n)]
    in_specs += [pl.BlockSpec((levels, rows, width), lambda i, me: (0, row_block[0], 0))] * n
    in_specs += [pl.BlockSpec((rows, width), lambda i, me: (row_block[0], 0))]
    out_specs = [pl.BlockSpec((step, levels, rows, width), lambda i, me: (i, 0, 0, 0))] * n
    out_shape = [jax.ShapeDtypeStruct((count, levels, rows, width), jnp.float32)] * n
    return call(
        kernel, (count // step,), in_specs, out_specs, out_shape, [adj] * n + list(rates) + [active], me,
        count * levels * rows * width * n,
    )


def coefficients(me, courant_lat, mass, entrain, cloud, north, n):
    levels, rows, width = mass.shape
    share = levels // n

    def kernel(me_ref, lat_ref, mass_ref, entrain_ref, cloud_ref, north_ref, rate_ref, inside_ref, detrain_ref):
        total = jnp.zeros((rows, width), jnp.float32)
        base, top = cloud_ref[0], cloud_ref[1]
        for r in range(n):
            owner = lax.rem(me_ref[0] - r + n, n)
            for l in range(share):
                level = owner * share + l
                inside = jnp.where((level >= base) & (level <= top), 1.0, 0.0)
                air = inside * mass_ref[level]
                total = total + air
                inside_ref[r * share + l] = inside
                detrain_ref[r * share + l] = air
                rate_ref[r * share + l] = lat_ref[level] * north_ref[...]
        factor = entrain_ref[...] / total
        for l in range(levels):
            detrain_ref[l] = detrain_ref[l] * factor

    full = pl.BlockSpec((levels, rows, width), lambda i, me: (0, 0, 0))
    flat = pl.BlockSpec((rows, width), lambda i, me: (0, 0))
    return call(
        kernel, (1,), [full, full, flat, pl.BlockSpec((2, rows, width), lambda i, me: (0, 0, 0)), flat],
        [full] * 3, [jax.ShapeDtypeStruct((levels, rows, width), jnp.float32)] * 3,
        [courant_lat, mass, entrain, cloud, north], me, levels * rows * width,
    )


def south_rows(me, tops, souths, step):
    n = len(tops)
    count, first, _, width = tops[0].shape
    rest = souths[0].shape[1]
    share = first + rest

    def kernel(me_ref, *refs):
        a, b, o = refs[:n], refs[n : 2 * n], refs[2 * n]

        def one(m, carry):
            for r in range(n):
                for l in range(first):
                    o[m, r * share + l : r * share + l + 1, :] = a[r][m, l, :1, :]
                for l in range(rest):
                    k = r * share + first + l
                    o[m, k : k + 1, :] = b[r][m, l, :1, :]
            return carry

        lax.fori_loop(0, step, one, 0)

    in_specs = [pl.BlockSpec((step, first, HALF, width), lambda i, me: (i, 0, 0, 0))] * n
    in_specs += [pl.BlockSpec((step, rest, HALF, width), lambda i, me: (i, 0, 0, 0))] * n
    return call(
        kernel, (count // step,), in_specs, pl.BlockSpec((step, n * share, width), lambda i, me: (i, 0, 0)),
        jax.ShapeDtypeStruct((count, n * share, width), jnp.float32), list(tops) + list(souths), me,
        count * n * share * width * HALF,
    )


def finish(me, out, first_moment, tops, souths, norths, edges, rate, inside, detrain, entrain, step):
    n = len(tops)
    total_moments, first, rows, width = tops[0].shape
    count, rest = norths[0].shape[:2]
    share = first + rest
    levels = n * share
    base = first_moment // step

    def kernel(me_ref, *refs):
        a, b, c = refs[:n], refs[n : 2 * n], refs[2 * n : 3 * n]
        edge_ref, rate_ref, inside_ref, detrain_ref, entrain_ref = refs[3 * n : 3 * n + 5]
        o = refs[-1]
        top_row = lax.broadcasted_iota(jnp.int32, (HALF, width), 0) == HALF - 1
        low, high = slice(0, HALF), slice(HALF, 2 * HALF)

        def one(m, carry):
            sums = [jnp.zeros((HALF, width), jnp.float32), jnp.zeros((HALF, width), jnp.float32)]
            for r in range(n):
                owner = lax.rem(me_ref[0] - r + n, n)
                for l in range(share):
                    k = r * share + l
                    if l < first:
                        f0, f1 = a[r][m, l, low, :], a[r][m, l, high, :]
                    else:
                        f0, f1 = b[r][m, l - first], c[r][m, l - first]
                    up0, up1 = pltpu.roll(f0, HALF - 1, 0), pltpu.roll(f1, HALF - 1, 0)
                    edge = jnp.broadcast_to(edge_ref[m, k : k + 1, :], (HALF, width))
                    n0, n1 = jnp.where(top_row, up1, up0), jnp.where(top_row, edge, up1)
                    m0 = f0 + rate_ref[k, low, :] * (n0 - f0)
                    m1 = f1 + rate_ref[k, high, :] * (n1 - f1)
                    sums[0] = sums[0] + inside_ref[k, low, :] * m0
                    sums[1] = sums[1] + inside_ref[k, high, :] * m1
                    o[m, owner * share + l, low, :] = m0
                    o[m, owner * share + l, high, :] = m1
            for r in range(n):
                owner = lax.rem(me_ref[0] - r + n, n)
                for l in range(share):
                    k = r * share + l
                    for part, whole in ((low, sums[0]), (high, sums[1])):
                        keep = 1.0 - entrain_ref[part, :] * inside_ref[k, part, :]
                        moved = o[m, owner * share + l, part, :]
                        o[m, owner * share + l, part, :] = keep * moved + detrain_ref[k, part, :] * whole
            return carry

        lax.fori_loop(0, step, one, 0)

    full = pl.BlockSpec((levels, rows, width), lambda i, me: (0, 0, 0))
    in_specs = [pl.BlockSpec((step, first, rows, width), lambda i, me: (i + base, 0, 0, 0))] * n
    in_specs += [pl.BlockSpec((step, rest, HALF, width), lambda i, me: (i + base, 0, 0, 0))] * n
    in_specs += [pl.BlockSpec((step, rest, HALF, width), lambda i, me: (i, 0, 0, 0))] * n
    in_specs += [pl.BlockSpec((step, levels, width), lambda i, me: (i + base, 0, 0))]
    in_specs += [full] * 3 + [pl.BlockSpec((rows, width), lambda i, me: (0, 0))]
    operands = list(tops) + list(souths) + list(norths) + [edges, rate, inside, detrain, entrain]
    aliases = None
    if out is not None:
        in_specs.append(pl.BlockSpec(memory_space=pl.ANY))
        operands.append(out)
        aliases = {len(operands): 0}
    return call(
        kernel, (count // step,), in_specs,
        pl.BlockSpec((step, levels, rows, width), lambda i, me: (i + base, 0, 0, 0)),
        jax.ShapeDtypeStruct((total_moments, levels, rows, width), jnp.float32), operands, me,
        count * levels * rows * width, aliases,
    )


CHUNKS = (8, 4, 2, 1, 1)


def body(adj_in, courant_lon, courant_lat, mass, entrain, cloud, substeps):
    n = lax.axis_size("lon")
    moments, share, rows, _ = adj_in.shape
    width = courant_lon.shape[2]
    position = lax.axis_index("lon").astype(jnp.int32)
    me = position[None]
    first, rest = 1, share - 1

    def rates_of(start, size, r):
        dest = lax.rem(position - r + n, n)
        block = lax.dynamic_slice_in_dim(courant_lon, dest * share + start, size, 0)
        return sent_east(block, n - r) if r else block

    active = jnp.broadcast_to(substeps[:, None], (rows, width))
    latitude = lax.axis_index("lat") * rows + jnp.arange(rows, dtype=jnp.int32)
    north = (latitude < rows * lax.axis_size("lat") - 1).astype(jnp.float32)
    north = jnp.broadcast_to(north[:, None], (rows, width))

    rates_a = [rates_of(0, first, r) for r in range(n)]
    rates_b = [rates_of(first, rest, r) for r in range(n)]

    def exchanged(blocks):
        return [blocks[0]] + [sent_east(blocks[r], r) for r in range(1, n)]

    tops = exchanged(sweep(me, adj_in, rates_a, active, (0, moments), 8, first, 0, (0, rows)))
    souths = exchanged(sweep(me, adj_in, rates_b, active, (0, moments), 4, share, first, (0, HALF)))
    norths, start = [], 0
    for size in CHUNKS:
        norths.append(
            exchanged(sweep(me, adj_in, rates_b, active, (start, size), min(size, 4), share, first, (1, HALF)))
        )
        start += size

    rate, inside, detrain = coefficients(me, courant_lat, mass, entrain, cloud, north, n)
    edges = sent_south(south_rows(me, tops, souths, 8))
    out, start = None, 0
    for size, chunk in zip(CHUNKS, norths):
        out = finish(
            me, out, start, tops, souths, chunk, edges, rate, inside, detrain, entrain, min(size, 2)
        )
        start += size
    return out


def solution(mesh):
    return jax.shard_map(
        body,
        mesh=mesh,
        in_specs=(
            P(None, "lon", "lat", None),
            P(None, "lat", "lon"),
            P(None, "lat", "lon"),
            P(None, "lat", "lon"),
            P("lat", "lon"),
            P(None, "lat", "lon"),
            P("lat"),
        ),
        out_specs=P(None, None, "lat", "lon"),
        check_vma=False,
    )
```

```python
import functools

import jax
import jax.numpy as jnp
from jax import lax
from jax.experimental import pallas as pl
from jax.experimental.pallas import tpu as pltpu
from jax.sharding import PartitionSpec as P

MAXSUB = 8
HALF = 8
VMEM_LIMIT = 12 * 1024 * 1024
COST = 1024
STENCIL_COST = 2 * 10**8
FIRST = 8
VMEM_WIDE = 50 * 1024 * 1024
NORTH_CHUNKS = (8, 6, 2)


def swapped(block, r):
    n = lax.axis_size("lon")
    return lax.ppermute(block, "lon", [(i, i ^ r) for i in range(n)])


def sent_west(block):
    n = lax.axis_size("lon")
    return lax.ppermute(block, "lon", [(i, (i - 1) % n) for i in range(n)])


def sent_south(block):
    n = lax.axis_size("lat")
    return lax.ppermute(block, "lat", [(i + 1, i) for i in range(n - 1)])


def f32(*shape):
    return jax.ShapeDtypeStruct(shape, jnp.float32)


SCALAR = pl.BlockSpec(memory_space=pltpu.SMEM)
NEAR = pl.BlockSpec(memory_space=pltpu.VMEM)
FAR = pl.BlockSpec(memory_space=pltpu.HBM)
ANY = pl.BlockSpec(memory_space=pl.ANY)


def call(kernel, in_specs, operands, out_specs, out_shape, flops, moved, aliases=None, scratch=(), limit=VMEM_LIMIT, grid=(), cost=None):
    return pl.pallas_call(
        kernel,
        in_specs=in_specs,
        out_specs=out_specs,
        out_shape=out_shape,
        grid=grid,
        scratch_shapes=list(scratch),
        input_output_aliases=aliases or {},
        compiler_params=pltpu.CompilerParams(vmem_limit_bytes=limit),
        cost_estimate=pl.CostEstimate(flops=min(flops, cost or COST), bytes_accessed=cost or min(moved, COST), transcendentals=0),
    )(*operands)


def tile_of(adj, me_ref, r, width, first, count, rows):
    start = pl.multiple_of((me_ref[0] ^ r) * width, width)
    return adj.at[pl.ds(first, count), :, rows, pl.ds(start, width)]


def held_for(block, token):
    def kernel(b, t, o):
        pass

    return call(kernel, [ANY, ANY], [block, token], ANY, f32(*block.shape), 0, 0, {0: 0})


def packed_rates(me, courant):
    levels, rows, width = courant.shape
    per = width // MAXSUB

    def kernel(c, o):
        lane = lax.broadcasted_iota(jnp.int32, (rows, width), 1)
        for b in range(levels // per):
            total = jnp.where(lane < MAXSUB, c[b * per], 0.0)
            for l in range(1, per):
                total = total + pltpu.roll(jnp.where(lane < MAXSUB, c[b * per + l], 0.0), MAXSUB * l, 1)
            o[b] = total

    size = levels * rows * width
    return call(kernel, [NEAR], [courant], NEAR, f32(levels // per, rows, width), size * 3, size * 4)


def taken(me, adj, width, parts, *tokens):
    share = adj.shape[1]

    def kernel(me_ref, a, *refs):
        outs, sems = refs[len(tokens) : -1], refs[-1]
        copies = [
            pltpu.make_async_copy(tile_of(a, me_ref, r, width, first, count, rows), o, sems.at[i])
            for i, ((r, first, count, rows), o) in enumerate(zip(parts, outs))
        ]
        for copy in copies:
            copy.start()
        for copy in copies:
            copy.wait()

    shapes = [f32(count, share, rows.stop - rows.start, width) for _, _, count, rows in parts]
    return call(
        kernel, [SCALAR, FAR] + [ANY] * len(tokens), [me, adj, *tokens], [NEAR] * len(shapes), shapes, 1024, 1024, None,
        [pltpu.SemaphoreType.DMA((len(parts),))], VMEM_WIDE,
    )


def prepared(me, adj, width, n, *tokens):
    moments, share, rows, _ = adj.shape
    step = 4
    many = n - 2
    extra = rows // HALF
    rest = moments - FIRST

    def kernel(me_ref, a, *refs):
        halo, near, *refs = refs[len(tokens) :]
        fars, (tiles, sems, tile_sems) = refs[:many], refs[many:]
        tile_copies = []
        for part in range(moments // step):
            for t in range(n):
                source = a.at[pl.ds(part * step, step), :, :, pl.ds(t * width, width)]
                copy = pltpu.make_async_copy(source, tiles.at[t, pl.ds(part * step, step)], tile_sems.at[part, t])
                copy.start()
                tile_copies.append(copy)
        pairs = [(tile_of(a, me_ref, 1, width, 0, moments, slice(0, rows)), near.at[pl.ds(0, moments)])]
        for r, far in enumerate(fars, 2):
            pairs.append((tile_of(a, me_ref, r, width, FIRST, rest, slice(0, HALF)), far.at[pl.ds(0, rest)]))
        copies = [pltpu.make_async_copy(source, o, sems.at[i]) for i, (source, o) in enumerate(pairs)]
        for copy in copies:
            copy.start()
        lane = lax.broadcasted_iota(jnp.int32, (share, rows, width), 2)
        for copy in tile_copies:
            copy.wait()
        for r in range(n):
            east = lax.rem((me_ref[0] ^ r) + 1, n)
            total = jnp.zeros((share, rows, width), jnp.float32)
            for m in range(moments):
                kept = jnp.where(lane < MAXSUB, tiles[east, m], 0.0)
                total = total + pltpu.roll(kept, MAXSUB * m, 2)
            if r == 0:
                halo[0] = total
            elif r == 1:
                near[moments] = total
            else:
                for g in range(extra):
                    fars[r - 2][rest + g] = total[:, g * HALF : (g + 1) * HALF, :]
        for copy in copies:
            copy.wait()

    shapes = [f32(1, share, rows, width), f32(moments + 1, share, rows, width)]
    shapes += [f32(rest + extra, share, HALF, width)] * many
    return call(
        kernel, [SCALAR, FAR] + [ANY] * len(tokens), [me, adj, *tokens], [NEAR] * len(shapes), shapes, 1024, 1024, None,
        [
            pltpu.VMEM((n, moments, share, rows, width), jnp.float32),
            pltpu.SemaphoreType.DMA((len(shapes),)),
            pltpu.SemaphoreType.DMA((moments // step, n)),
        ],
        VMEM_WIDE,
    )


def stencil(me, courant, halo, active, n, *tokens):
    levels, rows, width = courant.shape
    share = levels // n
    per = width // MAXSUB

    def kernel(me_ref, c_ref, h_ref, act_ref, *refs):
        w_ref, p_ref = refs[len(tokens) :]
        lane = lax.broadcasted_iota(jnp.int32, (rows, width), 1)
        act = act_ref[...]

        def one(k, carry):
            level = (me_ref[0] ^ (k // share)) * share + lax.rem(k, share)
            c = c_ref[level]
            east = h_ref[level // per]
            east = pltpu.roll(east, width - MAXSUB * lax.rem(level, per), 1)
            both = jnp.where(lane < MAXSUB, east, c)
            moved = [c]
            for j in range(1, MAXSUB):
                moved.append(
                    jnp.where(lane < width - MAXSUB, pltpu.roll(c, width - j, 1), pltpu.roll(both, width - j, 1))
                )
            w = [jnp.ones((rows, width), jnp.float32)]
            for s in range(MAXSUB):
                on = act > s
                rate = [jnp.where(on, x, 0.0) for x in moved[: s + 1]]
                new = [w[0] * (1.0 - rate[0])]
                for q in range(1, s + 1):
                    new.append(w[q] * (1.0 - rate[q]) + w[q - 1] * rate[q - 1])
                new.append(w[s] * rate[s])
                w = new
            for q in range(MAXSUB + 1):
                inner = lane < width - q
                x = jnp.where(inner, w[q], 0.0)
                w_ref[q, k] = x
                if q:
                    x = jnp.where(inner, 0.0, w[q])
                    reach = MAXSUB
                    while reach < width:
                        x = x + pltpu.roll(x, reach, 1)
                        reach *= 2
                    p_ref[q - 1, k] = x
            return carry

        lax.fori_loop(0, levels, one, 0, unroll=4)

    size = levels * rows * width
    return call(
        kernel, [SCALAR, NEAR, NEAR, NEAR] + [ANY] * len(tokens), [me, courant, halo, active, *tokens], [NEAR, NEAR],
        [f32(MAXSUB + 1, levels, rows, width), f32(MAXSUB, levels, rows, width)], size * 300, size * 80, cost=STENCIL_COST,
    )


def beyond(halos, packed, first):
    share, width = halos[0].shape[1], halos[0].shape[3]
    levels, rows = packed.shape[1:3]
    count = len(halos)

    def kernel(*refs):
        hs, p, o = refs[:count], refs[count], refs[-1]
        for r in range(count):
            to, part = slice(r * share, (r + 1) * share), slice((first + r) * share, (first + r + 1) * share)
            high = hs[r].shape[2]
            for g in range(rows // high):
                row = slice(g * high, (g + 1) * high)
                h = hs[r][g]
                total = p[MAXSUB - 1, part, row, :] * h
                for k in range(1, MAXSUB):
                    total = total + p[k - 1, part, row, :] * pltpu.roll(h, MAXSUB - k, 2)
                o[to, row, :] = total

    def block_of(h):
        extra = rows // h.shape[2]
        last = h.shape[0] // extra - 1
        return pl.BlockSpec((extra, share, h.shape[2], width), lambda i: (last, 0, 0, 0))

    size = count * share * rows * width
    return call(
        kernel, [block_of(h) for h in halos] + [pl.BlockSpec(packed.shape, lambda i: (0, 0, 0, 0))],
        list(halos) + [packed], pl.BlockSpec((count * share, rows, width), lambda i: (0, 0, 0)),
        f32(count * share, rows, width), size * 24, size * 40, grid=(1,),
    )


def coefficients(me, courant_lat, mass, entrain, cloud, north, n):
    levels, rows, width = mass.shape
    share = levels // n

    def kernel(me_ref, lat_ref, mass_ref, entrain_ref, cloud_ref, north_ref, rate_ref, inside_ref, detrain_ref):
        total = jnp.zeros((rows, width), jnp.float32)
        base, top = cloud_ref[0], cloud_ref[1]
        for r in range(n):
            for l in range(share):
                level = (me_ref[0] ^ r) * share + l
                inside = jnp.where((level >= base) & (level <= top), 1.0, 0.0)
                air = inside * mass_ref[level]
                total = total + air
                inside_ref[r * share + l] = inside
                detrain_ref[r * share + l] = air
                rate_ref[r * share + l] = lat_ref[level] * north_ref[...]
        factor = entrain_ref[...] / total
        for l in range(levels):
            detrain_ref[l] = detrain_ref[l] * factor

    size = levels * rows * width
    return call(
        kernel, [SCALAR] + [NEAR] * 5, [me, courant_lat, mass, entrain, cloud, north], [NEAR] * 3,
        [f32(levels, rows, width)] * 3, size * 10, size * 20,
    )


def stepped(a, weights):
    axis, width = a.ndim - 1, a.shape[-1]
    total = weights[0] * a
    for k in range(1, MAXSUB + 1):
        total = total + weights[k] * pltpu.roll(a, width - k, axis)
    return total


def added(packed, shift, past, step):
    return jnp.stack([jnp.where(past, pltpu.roll(packed, shift - MAXSUB * m, 1), 0.0) for m in range(step)])


def swept(me, blocks, first, weights, extra, start, moments, rows, step):
    count = len(blocks)
    levels, width = weights.shape[1], weights.shape[3]
    size = extra.shape[0]
    share = size // count

    def kernel(me_ref, *refs):
        a, (w_ref, x_ref, o, e) = refs[:count], refs[count:]
        past = lax.broadcasted_iota(jnp.int32, (HALF, width), 1) >= width - MAXSUB
        shift = width - MAXSUB - MAXSUB * (start + pl.program_id(0) * step)
        for g in range(rows // HALF):
            part = slice(g * HALF, (g + 1) * HALF)
            for r in range(count):
                for l in range(share):
                    k = r * share + l
                    x = stepped(a[r][:, l, part, :], [w_ref[q, first * share + k, part, :] for q in range(MAXSUB + 1)])
                    x = x + added(x_ref[k, part, :], shift, past, step)
                    o[:, k, part, :] = x
                    if g == 0:
                        e[:, k : k + 1, :] = x[:, :1, :]

    in_specs = [pl.BlockSpec((step, share, rows, width), index) for _, index in blocks]
    in_specs += [
        pl.BlockSpec((MAXSUB + 1, levels, rows, width), lambda i, me: (0, 0, 0, 0)),
        pl.BlockSpec((size, rows, width), lambda i, me: (0, 0, 0)),
    ]
    work = moments * size * rows * width
    return prefetched(
        kernel, (moments // step,), in_specs,
        [
            pl.BlockSpec((step, size, rows, width), lambda i, me: (i, 0, 0, 0)),
            pl.BlockSpec((step, size, width), lambda i, me: (i, 0, 0)),
        ],
        [f32(moments, size, rows, width), f32(moments, size, width)],
        [me] + [array for array, _ in blocks] + [weights, extra], work * 25, work * 8,
    )


def prefetched(kernel, grid, in_specs, out_specs, out_shape, operands, flops, moved, aliases=None):
    return pl.pallas_call(
        kernel,
        grid_spec=pltpu.PrefetchScalarGridSpec(num_scalar_prefetch=1, grid=grid, in_specs=in_specs, out_specs=out_specs),
        out_shape=out_shape,
        input_output_aliases=aliases or {},
        compiler_params=pltpu.CompilerParams(vmem_limit_bytes=VMEM_LIMIT),
        cost_estimate=pl.CostEstimate(flops=min(flops, COST), bytes_accessed=min(moved, COST), transcendentals=0),
    )(*operands)


def finish(me, out, first, count, close, low, offset, norths, weights, extra, edges, rate, inside, detrain, entrain, step):
    many = len(norths)
    n = many + 2
    levels, rows, width = rate.shape
    share = levels // n
    moments = close.shape[0]
    base = first // step
    low_base = (first - offset) // step

    def kernel(me_ref, close_ref, low_ref, *refs):
        a = refs[:many]
        w_ref, x_ref, e_close, e_far, rate_ref, inside_ref, detrain_ref, entrain_ref = refs[many : many + 8]
        o = refs[-1]
        top_row = lax.broadcasted_iota(jnp.int32, (step, HALF, width), 1) == HALF - 1
        past = lax.broadcasted_iota(jnp.int32, (HALF, width), 1) >= width - MAXSUB
        groups = (slice(0, HALF), slice(HALF, 2 * HALF))
        shift = width - MAXSUB - MAXSUB * (first + pl.program_id(0) * step)
        sums = [jnp.zeros((step, HALF, width), jnp.float32) for _ in groups]
        for r in range(n):
            owner = (me_ref[0] ^ r) * share
            for l in range(share):
                k = r * share + l
                if r < 2:
                    f = [close_ref[:, k, part, :] for part in groups]
                    edge = e_close[:, k : k + 1, :]
                else:
                    j = k - 2 * share
                    x = stepped(a[r - 2][:, l], [w_ref[q, k] for q in range(MAXSUB + 1)])
                    f = [low_ref[:, j], x + added(x_ref[j], shift, past, step)]
                    edge = e_far[:, j : j + 1, :]
                up = [pltpu.roll(x, HALF - 1, 1) for x in f]
                north = [
                    jnp.where(top_row, up[1], up[0]),
                    jnp.where(top_row, jnp.broadcast_to(edge, (step, HALF, width)), up[1]),
                ]
                for g, part in enumerate(groups):
                    moved = f[g] + rate_ref[k, part, :] * (north[g] - f[g])
                    sums[g] = sums[g] + inside_ref[k, part, :] * moved
                    o[:, owner + l, part, :] = moved
        for r in range(n):
            owner = (me_ref[0] ^ r) * share
            for l in range(share):
                k = r * share + l
                for g, part in enumerate(groups):
                    keep = 1.0 - entrain_ref[part, :] * inside_ref[k, part, :]
                    o[:, owner + l, part, :] = keep * o[:, owner + l, part, :] + detrain_ref[k, part, :] * sums[g]

    full = pl.BlockSpec((levels, rows, width), lambda i, me: (0, 0, 0))
    here = lambda i, me: (i + base, 0, 0, 0)
    in_specs = [
        pl.BlockSpec((step, 2 * share, rows, width), here),
        pl.BlockSpec((step, many * share, HALF, width), lambda i, me: (i + low_base, 0, 0, 0)),
    ]
    in_specs += [pl.BlockSpec((step, share, HALF, width), lambda i, me: (i, 0, 0, 0))] * many
    in_specs += [
        pl.BlockSpec((MAXSUB + 1, levels, HALF, width), lambda i, me: (0, 0, 1, 0)),
        pl.BlockSpec((many * share, HALF, width), lambda i, me: (0, 1, 0)),
        pl.BlockSpec((step, 2 * share, width), lambda i, me: (i + base, 0, 0)),
        pl.BlockSpec((step, many * share, width), lambda i, me: (i + low_base, 0, 0)),
    ]
    in_specs += [full] * 3 + [pl.BlockSpec((rows, width), lambda i, me: (0, 0))]
    operands = [me, close, low] + list(norths) + [weights, extra] + list(edges) + [rate, inside, detrain, entrain]
    aliases = None
    if out is not None:
        aliases = {len(operands): 0}
        in_specs.append(pl.BlockSpec(memory_space=pl.ANY))
        operands.append(out)
    work = count * levels * rows * width
    return prefetched(
        kernel, (count // step,), in_specs, pl.BlockSpec((step, levels, rows, width), here),
        f32(moments, levels, rows, width), operands, work * 30, work * 8, aliases,
    )


def body(adj_in, courant_lon, courant_lat, mass, entrain, cloud, substeps):
    n = lax.axis_size("lon")
    moments, share, rows, _ = adj_in.shape
    width = courant_lon.shape[2]
    me = lax.axis_index("lon").astype(jnp.int32)[None]
    partners = list(range(2, n))

    def exchanged(blocks):
        return [swapped(b, r) for b, r in zip(blocks, partners)]

    south, upper = slice(0, HALF), slice(HALF, 2 * HALF)
    rates = packed_rates(me, courant_lon)
    firsts = taken(me, adj_in, width, [(r, 0, FIRST, south) for r in partners], rates)
    rates = sent_west(rates)
    firsts = exchanged([held_for(b, rates) for b in firsts])
    own_halo, near, *rests = prepared(me, adj_in, width, n, firsts[0])
    near = swapped(near, 1)
    rests = exchanged(rests)

    active = jnp.broadcast_to(substeps[:, None], (rows, width))
    latitude = lax.axis_index("lat") * rows + jnp.arange(rows, dtype=jnp.int32)
    has_north = (latitude < rows * lax.axis_size("lat") - 1).astype(jnp.float32)
    has_north = jnp.broadcast_to(has_north[:, None], (rows, width))
    rate, inside, detrain = coefficients(me, courant_lat, mass, entrain, cloud, has_north, n)
    weights, packed = stencil(me, courant_lon, rates, active, n, rate, firsts[-1])

    whole = lambda i, me: (i, 0, 0, 0)
    extra = beyond([own_halo, near], packed, 0)
    blocks = [(adj_in, lambda i, me: (i, 0, 0, me[0])), (near, whole)]
    close, edge_close = swept(me, blocks, 0, weights, extra, 0, moments, rows, 4)
    edge_close = sent_south(edge_close)
    extra = beyond(rests, packed, 2)
    lows = []
    for start, size, arrays in ((0, FIRST, firsts), (FIRST, moments - FIRST, rests)):
        low, edge = swept(me, [(array, whole) for array in arrays], 2, weights, extra, start, size, HALF, 4)
        lows.append((low, start, sent_south(edge)))

    parts, start = [], 0
    for size in NORTH_CHUNKS:
        parts += [(r, start, size, upper) for r in partners]
        start += size
    sent = taken(me, adj_in, width, parts, firsts[-1])
    out, start = None, 0
    for i, size in enumerate(NORTH_CHUNKS):
        blocks = exchanged(sent[i * (n - 2) : (i + 1) * (n - 2)])
        low, offset, edge = lows[0] if start < FIRST else lows[1]
        out = finish(
            me, out, start, size, close, low, offset, blocks, weights, extra, [edge_close, edge],
            rate, inside, detrain, entrain, 2,
        )
        start += size
    return out


def solution(mesh):
    return jax.shard_map(
        body,
        mesh=mesh,
        in_specs=(
            P(None, "lon", "lat", None),
            P(None, "lat", "lon"),
            P(None, "lat", "lon"),
            P(None, "lat", "lon"),
            P("lat", "lon"),
            P(None, "lat", "lon"),
            P("lat"),
        ),
        out_specs=P(None, None, "lat", "lon"),
        check_vma=False,
    )
```

```python
import functools

import jax
import jax.numpy as jnp
from jax import lax
from jax.experimental import pallas as pl
from jax.experimental.pallas import tpu as pltpu
from jax.sharding import PartitionSpec as P

MAXSUB = 8
HALF = 8
VMEM_LIMIT = 12 * 1024 * 1024
COST = 1024
VMEM_WIDE = 50 * 1024 * 1024
NORTH_CHUNKS = (10, 4, 2)


def swapped(block, r):
    n = lax.axis_size("lon")
    return lax.ppermute(block, "lon", [(i, i ^ r) for i in range(n)])


def sent_west(block):
    n = lax.axis_size("lon")
    return lax.ppermute(block, "lon", [(i, (i - 1) % n) for i in range(n)])


def sent_south(block):
    n = lax.axis_size("lat")
    return lax.ppermute(block, "lat", [(i + 1, i) for i in range(n - 1)])


def f32(*shape):
    return jax.ShapeDtypeStruct(shape, jnp.float32)


SCALAR = pl.BlockSpec(memory_space=pltpu.SMEM)
NEAR = pl.BlockSpec(memory_space=pltpu.VMEM)
FAR = pl.BlockSpec(memory_space=pltpu.HBM)
ANY = pl.BlockSpec(memory_space=pl.ANY)


def call(kernel, in_specs, operands, out_specs, out_shape, flops, moved, aliases=None, scratch=(), limit=VMEM_LIMIT, grid=()):
    return pl.pallas_call(
        kernel,
        in_specs=in_specs,
        out_specs=out_specs,
        out_shape=out_shape,
        grid=grid,
        scratch_shapes=list(scratch),
        input_output_aliases=aliases or {},
        compiler_params=pltpu.CompilerParams(vmem_limit_bytes=limit),
        cost_estimate=pl.CostEstimate(flops=min(flops, COST), bytes_accessed=min(moved, COST), transcendentals=0),
    )(*operands)


def tile_of(adj, me_ref, r, width, first, count, rows):
    start = pl.multiple_of((me_ref[0] ^ r) * width, width)
    return adj.at[pl.ds(first, count), :, rows, pl.ds(start, width)]


def held_for(block, token):
    def kernel(b, t, o):
        pass

    return call(kernel, [ANY, ANY], [block, token], ANY, f32(*block.shape), 0, 0, {0: 0})


def taken(me, adj, width, parts, *tokens):
    share = adj.shape[1]

    def kernel(me_ref, a, *refs):
        outs, sems = refs[len(tokens) : -1], refs[-1]
        copies = [
            pltpu.make_async_copy(tile_of(a, me_ref, r, width, first, count, rows), o, sems.at[i])
            for i, ((r, first, count, rows), o) in enumerate(zip(parts, outs))
        ]
        for copy in copies:
            copy.start()
        for copy in copies:
            copy.wait()

    shapes = [f32(count, share, rows.stop - rows.start, width) for _, _, count, rows in parts]
    return call(
        kernel, [SCALAR, FAR] + [ANY] * len(tokens), [me, adj, *tokens], [NEAR] * len(shapes), shapes, 1024, 1024, None,
        [pltpu.SemaphoreType.DMA((len(parts),))], VMEM_WIDE,
    )


def packed_rates(courant, token):
    levels, rows, width = courant.shape
    per = width // MAXSUB

    def kernel(c, _, o):
        lane = lax.broadcasted_iota(jnp.int32, (rows, width), 1)
        for b in range(levels // per):
            total = jnp.where(lane < MAXSUB, c[b * per], 0.0)
            for l in range(1, per):
                total = total + pltpu.roll(jnp.where(lane < MAXSUB, c[b * per + l], 0.0), MAXSUB * l, 1)
            o[b] = total

    return call(kernel, [NEAR, ANY], [courant, token], NEAR, f32(levels // per, rows, width), 1024, 1024)


def prepared(me, adj, width, n):
    moments, share, rows, _ = adj.shape
    step = 4
    many = n - 2
    parts = moments // step
    low, high = slice(0, HALF), slice(HALF, 2 * HALF)

    def kernel(me_ref, a, halo, near, *refs):
        fars, (own, upper, found, sems) = refs[:many], refs[many:]
        pieces = [(0, slice(0, rows), own), (1, slice(0, rows), near)]
        for r in range(2, n):
            pieces += [(r, low, fars[r - 2]), (r, high, upper.at[r - 2])]
        copies = []
        for part in range(parts):
            for i, (r, row, ref) in enumerate(pieces):
                source = tile_of(a, me_ref, r, width, part * step, step, row)
                copies.append(pltpu.make_async_copy(source, ref.at[pl.ds(part * step, step)], sems.at[part, i]))
        for copy in copies:
            copy.start()

        totals = [jnp.zeros((share, row.stop - row.start, width), jnp.float32) for _, row, _ in pieces]
        for part in range(parts):
            for copy in copies[part * len(pieces) : (part + 1) * len(pieces)]:
                copy.wait()
            for i, (_, row, ref) in enumerate(pieces):
                lane = lax.broadcasted_iota(jnp.int32, totals[i].shape, 2)
                for m in range(part * step, (part + 1) * step):
                    kept = jnp.where(lane < MAXSUB, ref[m], 0.0)
                    totals[i] = totals[i] + (pltpu.roll(kept, MAXSUB * m, 2) if m else kept)
        for (r, row, _), total in zip(pieces, totals):
            west = lax.rem((me_ref[0] ^ r) + (n - 1), n) ^ me_ref[0]
            found[west, :, row, :] = total
        halo[0] = found[0]
        near[moments] = found[1]
        for r in range(2, n):
            for g in range(rows // HALF):
                fars[r - 2][moments + g] = found[r, :, g * HALF : (g + 1) * HALF, :]

    shapes = [f32(1, share, rows, width), f32(moments + 1, share, rows, width)]
    shapes += [f32(moments + rows // HALF, share, HALF, width)] * many
    return call(
        kernel, [SCALAR, FAR], [me, adj], [NEAR] * len(shapes), shapes, 1024, 1024, None,
        [
            pltpu.VMEM((moments, share, rows, width), jnp.float32),
            pltpu.VMEM((many, moments, share, HALF, width), jnp.float32),
            pltpu.VMEM((n, share, rows, width), jnp.float32),
            pltpu.SemaphoreType.DMA((parts, 2 + 2 * many)),
        ],
        VMEM_WIDE,
    )


def stencil(me, courant, halo, active, n):
    levels, rows, width = courant.shape
    share = levels // n
    per = width // MAXSUB

    def kernel(me_ref, c_ref, h_ref, act_ref, w_ref, p_ref):
        lane = lax.broadcasted_iota(jnp.int32, (rows, width), 1)
        act = act_ref[...]

        def one(k, carry):
            level = (me_ref[0] ^ (k // share)) * share + lax.rem(k, share)
            c = c_ref[level]
            east = h_ref[level // per]
            east = pltpu.roll(east, width - MAXSUB * lax.rem(level, per), 1)
            both = jnp.where(lane < MAXSUB, east, c)
            moved = [c]
            for j in range(1, MAXSUB):
                moved.append(
                    jnp.where(lane < width - MAXSUB, pltpu.roll(c, width - j, 1), pltpu.roll(both, width - j, 1))
                )
            w = [jnp.ones((rows, width), jnp.float32)]
            for s in range(MAXSUB):
                on = act > s
                rate = [jnp.where(on, x, 0.0) for x in moved[: s + 1]]
                new = [w[0] * (1.0 - rate[0])]
                for q in range(1, s + 1):
                    new.append(w[q] * (1.0 - rate[q]) + w[q - 1] * rate[q - 1])
                new.append(w[s] * rate[s])
                w = new
            for q in range(MAXSUB + 1):
                inner = lane < width - q
                x = jnp.where(inner, w[q], 0.0)
                w_ref[q, k] = x
                if q:
                    x = jnp.where(inner, 0.0, w[q])
                    reach = MAXSUB
                    while reach < width:
                        x = x + pltpu.roll(x, reach, 1)
                        reach *= 2
                    p_ref[q - 1, k] = x
            return carry

        lax.fori_loop(0, levels, one, 0, unroll=4)

    size = levels * rows * width
    return call(
        kernel, [SCALAR, NEAR, NEAR, NEAR], [me, courant, halo, active], [NEAR, NEAR],
        [f32(MAXSUB + 1, levels, rows, width), f32(MAXSUB, levels, rows, width)], size * 300, size * 80,
    )


def beyond(halos, packed, first, token):
    share, width = halos[0].shape[1], halos[0].shape[3]
    levels, rows = packed.shape[1:3]
    count = len(halos)

    def kernel(*refs):
        hs, p, o = refs[:count], refs[count], refs[-1]
        for r in range(count):
            to, part = slice(r * share, (r + 1) * share), slice((first + r) * share, (first + r + 1) * share)
            high = hs[r].shape[2]
            for g in range(rows // high):
                row = slice(g * high, (g + 1) * high)
                h = hs[r][g]
                total = p[MAXSUB - 1, part, row, :] * h
                for k in range(1, MAXSUB):
                    total = total + p[k - 1, part, row, :] * pltpu.roll(h, MAXSUB - k, 2)
                o[to, row, :] = total

    def block_of(h):
        extra = rows // h.shape[2]
        last = h.shape[0] // extra - 1
        return pl.BlockSpec((extra, share, h.shape[2], width), lambda i: (last, 0, 0, 0))

    size = count * share * rows * width
    return call(
        kernel, [block_of(h) for h in halos] + [pl.BlockSpec(packed.shape, lambda i: (0, 0, 0, 0)), ANY],
        list(halos) + [packed, token], pl.BlockSpec((count * share, rows, width), lambda i: (0, 0, 0)),
        f32(count * share, rows, width), size * 24, size * 40, grid=(1,),
    )


def coefficients(me, courant_lat, mass, entrain, cloud, north, n, token):
    levels, rows, width = mass.shape
    share = levels // n

    def kernel(me_ref, lat_ref, mass_ref, entrain_ref, cloud_ref, north_ref, _, rate_ref, inside_ref, detrain_ref):
        total = jnp.zeros((rows, width), jnp.float32)
        base, top = cloud_ref[0], cloud_ref[1]
        for r in range(n):
            for l in range(share):
                level = (me_ref[0] ^ r) * share + l
                inside = jnp.where((level >= base) & (level <= top), 1.0, 0.0)
                air = inside * mass_ref[level]
                total = total + air
                inside_ref[r * share + l] = inside
                detrain_ref[r * share + l] = air
                rate_ref[r * share + l] = lat_ref[level] * north_ref[...]
        factor = entrain_ref[...] / total
        for l in range(levels):
            detrain_ref[l] = detrain_ref[l] * factor

    size = levels * rows * width
    return call(
        kernel, [SCALAR] + [NEAR] * 5 + [ANY], [me, courant_lat, mass, entrain, cloud, north, token], [NEAR] * 3,
        [f32(levels, rows, width)] * 3, size * 10, size * 20,
    )


def stepped(a, weights):
    axis, width = a.ndim - 1, a.shape[-1]
    total = weights[0] * a
    for k in range(1, MAXSUB + 1):
        total = total + weights[k] * pltpu.roll(a, width - k, axis)
    return total


def added(packed, shift, past, step):
    return jnp.stack([jnp.where(past, pltpu.roll(packed, shift - MAXSUB * m, 1), 0.0) for m in range(step)])


def swept(me, blocks, first, weights, extra, start, moments, rows, step):
    count = len(blocks)
    levels, width = weights.shape[1], weights.shape[3]
    size = extra.shape[0]
    share = size // count

    def kernel(me_ref, *refs):
        a, (w_ref, x_ref, o, e) = refs[:count], refs[count:]
        past = lax.broadcasted_iota(jnp.int32, (HALF, width), 1) >= width - MAXSUB
        shift = width - MAXSUB - MAXSUB * (start + pl.program_id(0) * step)
        for g in range(rows // HALF):
            part = slice(g * HALF, (g + 1) * HALF)
            for r in range(count):
                for l in range(share):
                    k = r * share + l
                    x = stepped(a[r][:, l, part, :], [w_ref[q, first * share + k, part, :] for q in range(MAXSUB + 1)])
                    x = x + added(x_ref[k, part, :], shift, past, step)
                    o[:, k, part, :] = x
                    if g == 0:
                        e[:, k : k + 1, :] = x[:, :1, :]

    in_specs = [pl.BlockSpec((step, share, rows, width), index) for _, index in blocks]
    in_specs += [
        pl.BlockSpec((MAXSUB + 1, levels, rows, width), lambda i, me: (0, 0, 0, 0)),
        pl.BlockSpec((size, rows, width), lambda i, me: (0, 0, 0)),
    ]
    work = moments * size * rows * width
    return prefetched(
        kernel, (moments // step,), in_specs,
        [
            pl.BlockSpec((step, size, rows, width), lambda i, me: (i, 0, 0, 0)),
            pl.BlockSpec((step, size, width), lambda i, me: (i, 0, 0)),
        ],
        [f32(moments, size, rows, width), f32(moments, size, width)],
        [me] + [array for array, _ in blocks] + [weights, extra], work * 25, work * 8,
    )


def prefetched(kernel, grid, in_specs, out_specs, out_shape, operands, flops, moved, aliases=None):
    return pl.pallas_call(
        kernel,
        grid_spec=pltpu.PrefetchScalarGridSpec(num_scalar_prefetch=1, grid=grid, in_specs=in_specs, out_specs=out_specs),
        out_shape=out_shape,
        input_output_aliases=aliases or {},
        compiler_params=pltpu.CompilerParams(vmem_limit_bytes=VMEM_LIMIT),
        cost_estimate=pl.CostEstimate(flops=min(flops, COST), bytes_accessed=min(moved, COST), transcendentals=0),
    )(*operands)


def finish(me, out, first, count, close, low, offset, norths, weights, extra, edges, rate, inside, detrain, entrain, step):
    many = len(norths)
    n = many + 2
    levels, rows, width = rate.shape
    share = levels // n
    moments = close.shape[0]
    base = first // step
    low_base = (first - offset) // step

    def kernel(me_ref, close_ref, low_ref, *refs):
        a = refs[:many]
        w_ref, x_ref, e_close, e_far, rate_ref, inside_ref, detrain_ref, entrain_ref = refs[many : many + 8]
        o = refs[-1]
        top_row = lax.broadcasted_iota(jnp.int32, (step, HALF, width), 1) == HALF - 1
        past = lax.broadcasted_iota(jnp.int32, (HALF, width), 1) >= width - MAXSUB
        groups = (slice(0, HALF), slice(HALF, 2 * HALF))
        shift = width - MAXSUB - MAXSUB * (first + pl.program_id(0) * step)
        sums = [jnp.zeros((step, HALF, width), jnp.float32) for _ in groups]
        for r in range(n):
            owner = (me_ref[0] ^ r) * share
            for l in range(share):
                k = r * share + l
                if r < 2:
                    f = [close_ref[:, k, part, :] for part in groups]
                    edge = e_close[:, k : k + 1, :]
                else:
                    j = k - 2 * share
                    x = stepped(a[r - 2][:, l], [w_ref[q, k] for q in range(MAXSUB + 1)])
                    f = [low_ref[:, j], x + added(x_ref[j], shift, past, step)]
                    edge = e_far[:, j : j + 1, :]
                up = [pltpu.roll(x, HALF - 1, 1) for x in f]
                north = [
                    jnp.where(top_row, up[1], up[0]),
                    jnp.where(top_row, jnp.broadcast_to(edge, (step, HALF, width)), up[1]),
                ]
                for g, part in enumerate(groups):
                    moved = f[g] + rate_ref[k, part, :] * (north[g] - f[g])
                    sums[g] = sums[g] + inside_ref[k, part, :] * moved
                    o[:, owner + l, part, :] = moved
        for r in range(n):
            owner = (me_ref[0] ^ r) * share
            for l in range(share):
                k = r * share + l
                for g, part in enumerate(groups):
                    keep = 1.0 - entrain_ref[part, :] * inside_ref[k, part, :]
                    o[:, owner + l, part, :] = keep * o[:, owner + l, part, :] + detrain_ref[k, part, :] * sums[g]

    full = pl.BlockSpec((levels, rows, width), lambda i, me: (0, 0, 0))
    here = lambda i, me: (i + base, 0, 0, 0)
    in_specs = [
        pl.BlockSpec((step, 2 * share, rows, width), here),
        pl.BlockSpec((step, many * share, HALF, width), lambda i, me: (i + low_base, 0, 0, 0)),
    ]
    in_specs += [pl.BlockSpec((step, share, HALF, width), lambda i, me: (i, 0, 0, 0))] * many
    in_specs += [
        pl.BlockSpec((MAXSUB + 1, levels, HALF, width), lambda i, me: (0, 0, 1, 0)),
        pl.BlockSpec((many * share, HALF, width), lambda i, me: (0, 1, 0)),
        pl.BlockSpec((step, 2 * share, width), lambda i, me: (i + base, 0, 0)),
        pl.BlockSpec((step, many * share, width), lambda i, me: (i + low_base, 0, 0)),
    ]
    in_specs += [full] * 3 + [pl.BlockSpec((rows, width), lambda i, me: (0, 0))]
    operands = [me, close, low] + list(norths) + [weights, extra] + list(edges) + [rate, inside, detrain, entrain]
    aliases = None
    if out is not None:
        aliases = {len(operands): 0}
        in_specs.append(pl.BlockSpec(memory_space=pl.ANY))
        operands.append(out)
    work = count * levels * rows * width
    return prefetched(
        kernel, (count // step,), in_specs, pl.BlockSpec((step, levels, rows, width), here),
        f32(moments, levels, rows, width), operands, work * 30, work * 8, aliases,
    )


def body(adj_in, courant_lon, courant_lat, mass, entrain, cloud, substeps):
    n = lax.axis_size("lon")
    moments, share, rows, _ = adj_in.shape
    width = courant_lon.shape[2]
    me = lax.axis_index("lon").astype(jnp.int32)[None]
    partners = list(range(2, n))

    def exchanged(blocks):
        return [swapped(b, r) for b, r in zip(blocks, partners)]

    south, upper = slice(0, HALF), slice(HALF, 2 * HALF)
    own_halo, near, *souths = prepared(me, adj_in, width, n)
    rates = sent_west(packed_rates(courant_lon, own_halo))
    souths = exchanged([held_for(b, rates) for b in souths])
    near = swapped(near, 1)

    active = jnp.broadcast_to(substeps[:, None], (rows, width))
    latitude = lax.axis_index("lat") * rows + jnp.arange(rows, dtype=jnp.int32)
    has_north = (latitude < rows * lax.axis_size("lat") - 1).astype(jnp.float32)
    has_north = jnp.broadcast_to(has_north[:, None], (rows, width))
    weights, packed = stencil(me, courant_lon, rates, active, n)
    rate, inside, detrain = coefficients(me, courant_lat, mass, entrain, cloud, has_north, n, own_halo)

    whole = lambda i, me: (i, 0, 0, 0)
    extra = beyond([own_halo, near], packed, 0, rate)
    blocks = [(adj_in, lambda i, me: (i, 0, 0, me[0])), (near, whole)]
    close, edge_close = swept(me, blocks, 0, weights, extra, 0, moments, rows, 4)
    edge_close = sent_south(edge_close)
    extra = beyond(souths, packed, 2, rate)
    low, edge = swept(me, [(array, whole) for array in souths], 2, weights, extra, 0, moments, HALF, 4)
    edges = [edge_close, sent_south(edge)]

    parts, start = [], 0
    for size in NORTH_CHUNKS:
        parts += [(r, start, size, upper) for r in partners]
        start += size
    sent = taken(me, adj_in, width, parts, souths[0], edge_close)
    out, start = None, 0
    for i, size in enumerate(NORTH_CHUNKS):
        blocks = exchanged(sent[i * (n - 2) : (i + 1) * (n - 2)])
        out = finish(
            me, out, start, size, close, low, 0, blocks, weights, extra, edges,
            rate, inside, detrain, entrain, 2,
        )
        start += size
    return out


def solution(mesh):
    return jax.shard_map(
        body,
        mesh=mesh,
        in_specs=(
            P(None, "lon", "lat", None),
            P(None, "lat", "lon"),
            P(None, "lat", "lon"),
            P(None, "lat", "lon"),
            P("lat", "lon"),
            P(None, "lat", "lon"),
            P("lat"),
        ),
        out_specs=P(None, None, "lat", "lon"),
        check_vma=False,
    )
```

```python
import functools

import jax
import jax.numpy as jnp
from jax import lax
from jax.experimental import pallas as pl
from jax.experimental.pallas import tpu as pltpu
from jax.sharding import PartitionSpec as P

MAXSUB = 8
HALF = 8
VMEM_LIMIT = 12 * 1024 * 1024
COST = 1024
VMEM_WIDE = 50 * 1024 * 1024
FIRST = 4
NORTH_CHUNKS = (10, 4, 2)


def swapped(block, r):
    n = lax.axis_size("lon")
    return lax.ppermute(block, "lon", [(i, i ^ r) for i in range(n)])


def sent_west(block):
    n = lax.axis_size("lon")
    return lax.ppermute(block, "lon", [(i, (i - 1) % n) for i in range(n)])


def sent_south(block):
    n = lax.axis_size("lat")
    return lax.ppermute(block, "lat", [(i + 1, i) for i in range(n - 1)])


def f32(*shape):
    return jax.ShapeDtypeStruct(shape, jnp.float32)


SCALAR = pl.BlockSpec(memory_space=pltpu.SMEM)
NEAR = pl.BlockSpec(memory_space=pltpu.VMEM)
FAR = pl.BlockSpec(memory_space=pltpu.HBM)
ANY = pl.BlockSpec(memory_space=pl.ANY)


def call(kernel, in_specs, operands, out_specs, out_shape, flops, moved, aliases=None, scratch=(), limit=VMEM_LIMIT, grid=()):
    return pl.pallas_call(
        kernel,
        in_specs=in_specs,
        out_specs=out_specs,
        out_shape=out_shape,
        grid=grid,
        scratch_shapes=list(scratch),
        input_output_aliases=aliases or {},
        compiler_params=pltpu.CompilerParams(vmem_limit_bytes=limit),
        cost_estimate=pl.CostEstimate(flops=min(flops, COST), bytes_accessed=min(moved, COST), transcendentals=0),
    )(*operands)


def tile_of(adj, me_ref, r, width, first, count, rows):
    start = pl.multiple_of((me_ref[0] ^ r) * width, width)
    return adj.at[pl.ds(first, count), :, rows, pl.ds(start, width)]


def held_for(block, *tokens):
    def kernel(*refs):
        pass

    return call(kernel, [ANY] * (1 + len(tokens)), [block, *tokens], ANY, f32(*block.shape), 0, 0, {0: 0})


def taken(me, adj, width, parts, *tokens):
    share = adj.shape[1]

    def kernel(me_ref, a, *refs):
        outs, sems = refs[len(tokens) : -1], refs[-1]
        copies = [
            pltpu.make_async_copy(tile_of(a, me_ref, r, width, first, count, rows), o, sems.at[i])
            for i, ((r, first, count, rows), o) in enumerate(zip(parts, outs))
        ]
        for copy in copies:
            copy.start()
        for copy in copies:
            copy.wait()

    shapes = [f32(count, share, rows.stop - rows.start, width) for _, _, count, rows in parts]
    return call(
        kernel, [SCALAR, FAR] + [ANY] * len(tokens), [me, adj, *tokens], [NEAR] * len(shapes), shapes, 1024, 1024, None,
        [pltpu.SemaphoreType.DMA((len(parts),))], VMEM_WIDE,
    )


def packed_rates(courant, token):
    levels, rows, width = courant.shape
    per = width // MAXSUB

    def kernel(c, _, o):
        lane = lax.broadcasted_iota(jnp.int32, (rows, width), 1)
        for b in range(levels // per):
            total = jnp.where(lane < MAXSUB, c[b * per], 0.0)
            for l in range(1, per):
                total = total + pltpu.roll(jnp.where(lane < MAXSUB, c[b * per + l], 0.0), MAXSUB * l, 1)
            o[b] = total

    return call(kernel, [NEAR, ANY], [courant, token], NEAR, f32(levels // per, rows, width), 1024, 1024)


def prepared(me, adj, width, n):
    moments, share, rows, _ = adj.shape
    step = FIRST
    many = n - 2
    parts = moments // step
    rest = moments - FIRST
    low, high = slice(0, HALF), slice(HALF, 2 * HALF)

    def kernel(me_ref, a, halo, near, *refs):
        fars, (own, upper, early, found, sems) = refs[:many], refs[many:]

        def block_of(ref, r, part):
            if ref is None:
                return early.at[r - 2] if part == 0 else fars[r - 2].at[pl.ds((part - 1) * step, step)]
            return ref.at[pl.ds(part * step, step)]

        pieces = [(0, slice(0, rows), own), (1, slice(0, rows), near)]
        for r in range(2, n):
            pieces += [(r, low, None), (r, high, upper.at[r - 2])]
        copies = []
        for part in range(parts):
            for i, (r, row, ref) in enumerate(pieces):
                source = tile_of(a, me_ref, r, width, part * step, step, row)
                copies.append(pltpu.make_async_copy(source, block_of(ref, r, part), sems.at[part, i]))
        for copy in copies:
            copy.start()

        totals = [jnp.zeros((share, row.stop - row.start, width), jnp.float32) for _, row, _ in pieces]
        for part in range(parts):
            for copy in copies[part * len(pieces) : (part + 1) * len(pieces)]:
                copy.wait()
            for i, (r, row, ref) in enumerate(pieces):
                lane = lax.broadcasted_iota(jnp.int32, totals[i].shape, 2)
                block = block_of(ref, r, part)
                for m in range(part * step, (part + 1) * step):
                    kept = jnp.where(lane < MAXSUB, block[m - part * step], 0.0)
                    totals[i] = totals[i] + (pltpu.roll(kept, MAXSUB * m, 2) if m else kept)
        for (r, row, _), total in zip(pieces, totals):
            west = lax.rem((me_ref[0] ^ r) + (n - 1), n) ^ me_ref[0]
            found[west, :, row, :] = total
        halo[0] = found[0]
        near[moments] = found[1]
        for r in range(2, n):
            for g in range(rows // HALF):
                fars[r - 2][rest + g] = found[r, :, g * HALF : (g + 1) * HALF, :]

    shapes = [f32(1, share, rows, width), f32(moments + 1, share, rows, width)]
    shapes += [f32(rest + rows // HALF, share, HALF, width)] * many
    return call(
        kernel, [SCALAR, FAR], [me, adj], [NEAR] * len(shapes), shapes, 1024, 1024, None,
        [
            pltpu.VMEM((moments, share, rows, width), jnp.float32),
            pltpu.VMEM((many, moments, share, HALF, width), jnp.float32),
            pltpu.VMEM((many, FIRST, share, HALF, width), jnp.float32),
            pltpu.VMEM((n, share, rows, width), jnp.float32),
            pltpu.SemaphoreType.DMA((parts, 2 + 2 * many)),
        ],
        VMEM_WIDE,
    )


def stencil(me, courant, halo, active, n):
    levels, rows, width = courant.shape
    share = levels // n
    per = width // MAXSUB

    def kernel(me_ref, c_ref, h_ref, act_ref, w_ref, p_ref):
        lane = lax.broadcasted_iota(jnp.int32, (rows, width), 1)
        act = act_ref[...]

        def one(k, carry):
            level = (me_ref[0] ^ (k // share)) * share + lax.rem(k, share)
            c = c_ref[level]
            east = h_ref[level // per]
            east = pltpu.roll(east, width - MAXSUB * lax.rem(level, per), 1)
            both = jnp.where(lane < MAXSUB, east, c)
            moved = [c]
            for j in range(1, MAXSUB):
                moved.append(
                    jnp.where(lane < width - MAXSUB, pltpu.roll(c, width - j, 1), pltpu.roll(both, width - j, 1))
                )
            w = [jnp.ones((rows, width), jnp.float32)]
            for s in range(MAXSUB):
                on = act > s
                rate = [jnp.where(on, x, 0.0) for x in moved[: s + 1]]
                new = [w[0] * (1.0 - rate[0])]
                for q in range(1, s + 1):
                    new.append(w[q] * (1.0 - rate[q]) + w[q - 1] * rate[q - 1])
                new.append(w[s] * rate[s])
                w = new
            for q in range(MAXSUB + 1):
                inner = lane < width - q
                x = jnp.where(inner, w[q], 0.0)
                w_ref[q, k] = x
                if q:
                    x = jnp.where(inner, 0.0, w[q])
                    reach = MAXSUB
                    while reach < width:
                        x = x + pltpu.roll(x, reach, 1)
                        reach *= 2
                    p_ref[q - 1, k] = x
            return carry

        lax.fori_loop(0, levels, one, 0, unroll=4)

    size = levels * rows * width
    return call(
        kernel, [SCALAR, NEAR, NEAR, NEAR], [me, courant, halo, active], [NEAR, NEAR],
        [f32(MAXSUB + 1, levels, rows, width), f32(MAXSUB, levels, rows, width)], size * 300, size * 80,
    )


def beyond(halos, packed, first, token):
    share, width = halos[0].shape[1], halos[0].shape[3]
    levels, rows = packed.shape[1:3]
    count = len(halos)

    def kernel(*refs):
        hs, p, o = refs[:count], refs[count], refs[-1]
        for r in range(count):
            to, part = slice(r * share, (r + 1) * share), slice((first + r) * share, (first + r + 1) * share)
            high = hs[r].shape[2]
            for g in range(rows // high):
                row = slice(g * high, (g + 1) * high)
                h = hs[r][g]
                total = p[MAXSUB - 1, part, row, :] * h
                for k in range(1, MAXSUB):
                    total = total + p[k - 1, part, row, :] * pltpu.roll(h, MAXSUB - k, 2)
                o[to, row, :] = total

    def block_of(h):
        extra = rows // h.shape[2]
        last = h.shape[0] // extra - 1
        return pl.BlockSpec((extra, share, h.shape[2], width), lambda i: (last, 0, 0, 0))

    size = count * share * rows * width
    return call(
        kernel, [block_of(h) for h in halos] + [pl.BlockSpec(packed.shape, lambda i: (0, 0, 0, 0)), ANY],
        list(halos) + [packed, token], pl.BlockSpec((count * share, rows, width), lambda i: (0, 0, 0)),
        f32(count * share, rows, width), size * 24, size * 40, grid=(1,),
    )


def coefficients(me, courant_lat, mass, entrain, cloud, north, n, token):
    levels, rows, width = mass.shape
    share = levels // n

    def kernel(me_ref, lat_ref, mass_ref, entrain_ref, cloud_ref, north_ref, _, rate_ref, inside_ref, detrain_ref):
        total = jnp.zeros((rows, width), jnp.float32)
        base, top = cloud_ref[0], cloud_ref[1]
        for r in range(n):
            for l in range(share):
                level = (me_ref[0] ^ r) * share + l
                inside = jnp.where((level >= base) & (level <= top), 1.0, 0.0)
                air = inside * mass_ref[level]
                total = total + air
                inside_ref[r * share + l] = inside
                detrain_ref[r * share + l] = air
                rate_ref[r * share + l] = lat_ref[level] * north_ref[...]
        factor = entrain_ref[...] / total
        for l in range(levels):
            detrain_ref[l] = detrain_ref[l] * factor

    size = levels * rows * width
    return call(
        kernel, [SCALAR] + [NEAR] * 5 + [ANY], [me, courant_lat, mass, entrain, cloud, north, token], [NEAR] * 3,
        [f32(levels, rows, width)] * 3, size * 10, size * 20,
    )


def stepped(a, weights):
    axis, width = a.ndim - 1, a.shape[-1]
    total = weights[0] * a
    for k in range(1, MAXSUB + 1):
        total = total + weights[k] * pltpu.roll(a, width - k, axis)
    return total


def added(packed, shift, past, step):
    return jnp.stack([jnp.where(past, pltpu.roll(packed, shift - MAXSUB * m, 1), 0.0) for m in range(step)])


def swept(me, blocks, first, weights, extra, start, moments, rows, step, heads=()):
    count = len(blocks)
    levels, width = weights.shape[1], weights.shape[3]
    size = extra.shape[0]
    share = size // count

    def kernel(me_ref, *refs):
        a, h, (w_ref, x_ref, o, e) = refs[:count], refs[count : count + len(heads)], refs[count + len(heads) :]
        head = pl.program_id(0) == 0
        past = lax.broadcasted_iota(jnp.int32, (HALF, width), 1) >= width - MAXSUB
        shift = width - MAXSUB - MAXSUB * (start + pl.program_id(0) * step)
        for g in range(rows // HALF):
            part = slice(g * HALF, (g + 1) * HALF)
            for r in range(count):
                for l in range(share):
                    k = r * share + l
                    x = a[r][:, l, part, :]
                    if heads:
                        x = jnp.where(head, h[r][:, l, part, :], x)
                    x = stepped(x, [w_ref[q, first * share + k, part, :] for q in range(MAXSUB + 1)])
                    x = x + added(x_ref[k, part, :], shift, past, step)
                    o[:, k, part, :] = x
                    if g == 0:
                        e[:, k : k + 1, :] = x[:, :1, :]

    in_specs = [pl.BlockSpec((step, share, rows, width), index) for _, index in blocks]
    in_specs += [pl.BlockSpec((step, share, rows, width), lambda i, me: (0, 0, 0, 0))] * len(heads)
    in_specs += [
        pl.BlockSpec((MAXSUB + 1, levels, rows, width), lambda i, me: (0, 0, 0, 0)),
        pl.BlockSpec((size, rows, width), lambda i, me: (0, 0, 0)),
    ]
    work = moments * size * rows * width
    return prefetched(
        kernel, (moments // step,), in_specs,
        [
            pl.BlockSpec((step, size, rows, width), lambda i, me: (i, 0, 0, 0)),
            pl.BlockSpec((step, size, width), lambda i, me: (i, 0, 0)),
        ],
        [f32(moments, size, rows, width), f32(moments, size, width)],
        [me] + [array for array, _ in blocks] + list(heads) + [weights, extra], work * 25, work * 8,
    )


def prefetched(kernel, grid, in_specs, out_specs, out_shape, operands, flops, moved, aliases=None):
    return pl.pallas_call(
        kernel,
        grid_spec=pltpu.PrefetchScalarGridSpec(num_scalar_prefetch=1, grid=grid, in_specs=in_specs, out_specs=out_specs),
        out_shape=out_shape,
        input_output_aliases=aliases or {},
        compiler_params=pltpu.CompilerParams(vmem_limit_bytes=VMEM_LIMIT),
        cost_estimate=pl.CostEstimate(flops=min(flops, COST), bytes_accessed=min(moved, COST), transcendentals=0),
    )(*operands)


def finish(me, out, first, count, close, low, offset, norths, weights, extra, edges, rate, inside, detrain, entrain, step):
    many = len(norths)
    n = many + 2
    levels, rows, width = rate.shape
    share = levels // n
    moments = close.shape[0]
    base = first // step
    low_base = (first - offset) // step

    def kernel(me_ref, close_ref, low_ref, *refs):
        a = refs[:many]
        w_ref, x_ref, e_close, e_far, rate_ref, inside_ref, detrain_ref, entrain_ref = refs[many : many + 8]
        o = refs[-1]
        top_row = lax.broadcasted_iota(jnp.int32, (step, HALF, width), 1) == HALF - 1
        past = lax.broadcasted_iota(jnp.int32, (HALF, width), 1) >= width - MAXSUB
        groups = (slice(0, HALF), slice(HALF, 2 * HALF))
        shift = width - MAXSUB - MAXSUB * (first + pl.program_id(0) * step)
        sums = [jnp.zeros((step, HALF, width), jnp.float32) for _ in groups]
        for r in range(n):
            owner = (me_ref[0] ^ r) * share
            for l in range(share):
                k = r * share + l
                if r < 2:
                    f = [close_ref[:, k, part, :] for part in groups]
                    edge = e_close[:, k : k + 1, :]
                else:
                    j = k - 2 * share
                    x = stepped(a[r - 2][:, l], [w_ref[q, k] for q in range(MAXSUB + 1)])
                    f = [low_ref[:, j], x + added(x_ref[j], shift, past, step)]
                    edge = e_far[:, j : j + 1, :]
                up = [pltpu.roll(x, HALF - 1, 1) for x in f]
                north = [
                    jnp.where(top_row, up[1], up[0]),
                    jnp.where(top_row, jnp.broadcast_to(edge, (step, HALF, width)), up[1]),
                ]
                for g, part in enumerate(groups):
                    moved = f[g] + rate_ref[k, part, :] * (north[g] - f[g])
                    sums[g] = sums[g] + inside_ref[k, part, :] * moved
                    o[:, owner + l, part, :] = moved
        for r in range(n):
            owner = (me_ref[0] ^ r) * share
            for l in range(share):
                k = r * share + l
                for g, part in enumerate(groups):
                    keep = 1.0 - entrain_ref[part, :] * inside_ref[k, part, :]
                    o[:, owner + l, part, :] = keep * o[:, owner + l, part, :] + detrain_ref[k, part, :] * sums[g]

    full = pl.BlockSpec((levels, rows, width), lambda i, me: (0, 0, 0))
    here = lambda i, me: (i + base, 0, 0, 0)
    in_specs = [
        pl.BlockSpec((step, 2 * share, rows, width), here),
        pl.BlockSpec((step, many * share, HALF, width), lambda i, me: (i + low_base, 0, 0, 0)),
    ]
    in_specs += [pl.BlockSpec((step, share, HALF, width), lambda i, me: (i, 0, 0, 0))] * many
    in_specs += [
        pl.BlockSpec((MAXSUB + 1, levels, HALF, width), lambda i, me: (0, 0, 1, 0)),
        pl.BlockSpec((many * share, HALF, width), lambda i, me: (0, 1, 0)),
        pl.BlockSpec((step, 2 * share, width), lambda i, me: (i + base, 0, 0)),
        pl.BlockSpec((step, many * share, width), lambda i, me: (i + low_base, 0, 0)),
    ]
    in_specs += [full] * 3 + [pl.BlockSpec((rows, width), lambda i, me: (0, 0))]
    operands = [me, close, low] + list(norths) + [weights, extra] + list(edges) + [rate, inside, detrain, entrain]
    aliases = None
    if out is not None:
        aliases = {len(operands): 0}
        in_specs.append(pl.BlockSpec(memory_space=pl.ANY))
        operands.append(out)
    work = count * levels * rows * width
    return prefetched(
        kernel, (count // step,), in_specs, pl.BlockSpec((step, levels, rows, width), here),
        f32(moments, levels, rows, width), operands, work * 30, work * 8, aliases,
    )


def body(adj_in, courant_lon, courant_lat, mass, entrain, cloud, substeps):
    n = lax.axis_size("lon")
    moments, share, rows, _ = adj_in.shape
    width = courant_lon.shape[2]
    me = lax.axis_index("lon").astype(jnp.int32)[None]
    partners = list(range(2, n))

    def exchanged(blocks):
        return [swapped(b, r) for b, r in zip(blocks, partners)]

    south, upper = slice(0, HALF), slice(HALF, 2 * HALF)
    firsts = exchanged(taken(me, adj_in, width, [(r, 0, FIRST, south) for r in partners]))
    rates = sent_west(packed_rates(courant_lon, me))
    own_halo, near, *souths = prepared(me, adj_in, width, n)
    near = swapped(held_for(near, rates, *firsts), 1)
    souths = exchanged([held_for(b, rates, *firsts) for b in souths])

    active = jnp.broadcast_to(substeps[:, None], (rows, width))
    latitude = lax.axis_index("lat") * rows + jnp.arange(rows, dtype=jnp.int32)
    has_north = (latitude < rows * lax.axis_size("lat") - 1).astype(jnp.float32)
    has_north = jnp.broadcast_to(has_north[:, None], (rows, width))
    weights, packed = stencil(me, courant_lon, rates, active, n)
    rate, inside, detrain = coefficients(me, courant_lat, mass, entrain, cloud, has_north, n, own_halo)

    whole = lambda i, me: (i, 0, 0, 0)
    extra = beyond([own_halo, near], packed, 0, rate)
    blocks = [(adj_in, lambda i, me: (i, 0, 0, me[0])), (near, whole)]
    close, edge_close = swept(me, blocks, 0, weights, extra, 0, moments, rows, 4)
    edge_close = sent_south(edge_close)
    extra = beyond(souths, packed, 2, edge_close)
    later = lambda i, me: (jnp.maximum(i - 1, 0), 0, 0, 0)
    low, edge = swept(me, [(array, later) for array in souths], 2, weights, extra, 0, moments, HALF, FIRST, firsts)
    edges = [edge_close, sent_south(edge)]

    parts, start = [], 0
    for size in NORTH_CHUNKS:
        parts += [(r, start, size, upper) for r in partners]
        start += size
    sent = taken(me, adj_in, width, parts, souths[0], close)
    out, start = None, 0
    for i, size in enumerate(NORTH_CHUNKS):
        blocks = exchanged(sent[i * (n - 2) : (i + 1) * (n - 2)])
        out = finish(
            me, out, start, size, close, low, 0, blocks, weights, extra, edges,
            rate, inside, detrain, entrain, 2,
        )
        start += size
    return out


def solution(mesh):
    return jax.shard_map(
        body,
        mesh=mesh,
        in_specs=(
            P(None, "lon", "lat", None),
            P(None, "lat", "lon"),
            P(None, "lat", "lon"),
            P(None, "lat", "lon"),
            P("lat", "lon"),
            P(None, "lat", "lon"),
            P("lat"),
        ),
        out_specs=P(None, None, "lat", "lon"),
        check_vma=False,
    )
```
